32 devices in a mesh: parts: 2 (over y), tensor: 4 (over z), group: 2 (over x), rep: 2 (over core).
Axes of the slice: x: 2, y: 2, z: 4, core: 2. Of those that a mesh axis runs over, the one named last changes fastest.
Arguments:
- hidden_rows: bfloat16 [512, 28672], P(('parts', 'tensor'), ('group', 'rep')), parts along dimension 0, may hold values from -6 to 6
- down_weight: bfloat16 [28672, 8192], P(('group', 'rep'), 'tensor'), may hold values from -0.03125 to 0.03125
- adapter_down: bfloat16 [8, 28672, 64], P('tensor', ('group', 'rep')), may hold values from -0.03125 to 0.03125
- adapter_up: bfloat16 [8, 64, 8192], P(('group', 'rep'), None, 'tensor'), may hold values from -0.75 to 0.75
- adapter_id: int32 [512, 1], P('parts'), parts along dimension 0, may hold values from 0 to 7; in each aligned block of 256 rows (0 to 255, 256 to 511, ...) at most 128 rows name the same one
- adapter_slot: int32 [8], replicated, may hold values from 0 to 7, each once
Outputs:
- scored: bfloat16 [512, 8192], P(('parts', 'group', 'rep'), 'tensor'), parts along dimension 0
The draws below stay inside these ranges and needn't reach their ends.
There are 2 independent parts, one for each index of `parts`. The reference program is written for one: setup_inputs(seed, part) draws one part's arguments, and reference() takes and returns one part's arrays. A program takes and returns all parts, laid end to end along the dimension named above; an argument that names none is the same for every part. Nothing has to cross between parts.
Inputs may be any that keep to these rules, and one draw needn't show every extreme that they name: `adapter_id`: at most 128 rows of one part name the same adapter, every row names one adapter, and every adapter is named by some row. A permutation: adapter a's factors lie at index adapter_slot[a] of adapter_down and adapter_up.
All inputs are finite; a program needn't handle non-finite values.
Results may differ from the reference program's by a relative error of at most 0.0032.
Values may be sent and summed in bfloat16 or wider, within the bound.
A program may use at most 128 MiB of HBM per device.

```python
import math
import jax
import jax.numpy as jnp
import numpy as np
from jax import lax

D = 8192
FF = 28672
RANK = 64
ADAPTERS = 8
ROWS = 256
CAP = 128


def block_levels(own_key, dims, split, least, top_value):
    factor_of, own = 1.0, jax.random.fold_in(own_key, 6)
    for dim, blocks in split:
        steps = jnp.exp(jax.random.uniform(jax.random.fold_in(own, dim), (blocks,), jnp.float32, least / len(split), top_value / len(split)))
        factor_of = factor_of * jnp.repeat(steps, dims[dim] // blocks).reshape([-1 if axis == dim else 1 for axis in range(len(dims))])
    return factor_of


def shared_out(rng, own, number, rows, number_of, top, most, lean):
    order = jax.random.permutation(rng, number_of)
    heavy_load, ordinary = portions_of(number_of, rows * top, most, lean, True), portions_of(number_of, rows * top, most, lean, False)
    places = jnp.arange(number_of)

    def named(sizes, rotation):
        used = int((sizes > 0).sum())
        fixed = max(1, used // 4)
        passed = fixed + (places - fixed + rotation * (used - fixed)) % max(1, number_of - fixed)
        return jnp.zeros((number_of,), jnp.int32).at[order[jnp.where(places < fixed, places, passed)]].set(jnp.asarray(sizes, jnp.int32))

    sizes = jnp.where(number % 4 == 0, named(heavy_load, number // 4), named(ordinary, number - number // 4 - 1))
    mixed = jax.random.permutation(jax.random.fold_in(own, 3), number_of)
    donor, taker = mixed[0:number_of // 2 * 2:2], mixed[1:number_of // 2 * 2:2]
    margin = jnp.minimum(sizes[donor] - 1, most - sizes[taker]) // 2
    margin = jnp.where((donor == order[0]) | (taker == order[0]) | (sizes[taker] == 0), 0, jnp.maximum(margin, 0))
    passed = jax.random.randint(jax.random.fold_in(own, 4), (number_of // 2,), 0, 1 << 20) % (margin + 1)
    sizes = sizes.at[donor].add(-passed).at[taker].add(passed)
    items = jnp.searchsorted(jnp.cumsum(sizes), jnp.arange(rows * top), side="right").astype(jnp.int32)
    table = items.reshape(top, rows).T
    table = table[jax.random.permutation(jax.random.fold_in(own, 1), rows)]
    rotation = jax.random.randint(jax.random.fold_in(own, 2), (rows, 1), 0, top)
    return jnp.take_along_axis(table, (jnp.arange(top)[None, :] + rotation) % top, axis=1)


def portions_of(count, total, bound, skew, full):
    loads = [(1 << 20) // math.isqrt(standing ** skew) + 1 for standing in range(1, count + 1)]
    largest = bound if full else min(bound, max(-(-total // count), total * loads[0] // sum(loads)))
    least = 1 if total - largest >= count - 1 else 0
    holding, spare = [largest] + [least] * (count - 1), total - largest - least * (count - 1)
    while spare > 0:
        movable = [i for i in range(1, count) if holding[i] < largest] or [i for i in range(1, count) if holding[i] < bound]
        whole, budget = sum([loads[i] for i in movable]), spare
        for i in movable:
            extra = min(bound - holding[i], max(1, budget * loads[i] // whole), spare)
            holding[i] = holding[i] + extra
            spare = spare - extra
    return np.array(holding)


def normal_values(stream_key, shape, spread, limit, cuts=(), held_as=jnp.bfloat16):
    array = jax.random.normal(stream_key, shape, jnp.float32) * spread
    if len(cuts) > 0:
        array = block_levels(stream_key, shape, cuts, -0.22, 0.18) * array
    return jnp.clip(array, min=-limit, max=limit).astype(held_as)


def setup_inputs(seed: int = 0, part: int = 0) -> dict:
    arg_keys = jax.random.split(jax.random.key(seed), 7)
    own_keys = jax.random.split(jax.random.fold_in(arg_keys[6], part), 7)
    hidden_rows = normal_values(own_keys[0], (ROWS, FF), 1.0, 6.0, ((0, 4), (1, 4)))
    down_weight = normal_values(arg_keys[1], (FF, D), FF ** -0.5, 0.03125, ((0, 4), (1, 4)))
    adapter_down = normal_values(arg_keys[2], (ADAPTERS, FF, RANK), FF ** -0.5, 0.03125, ((0, 4), (1, 4)))
    adapter_up = normal_values(arg_keys[3], (ADAPTERS, RANK, D), RANK ** -0.5, 0.75, ((0, 4), (2, 4)))
    adapter_id_keys = jax.random.split(jax.random.fold_in(own_keys[4], 1), ROWS // ROWS)
    adapter_id_turns = jax.random.permutation(jax.random.fold_in(own_keys[4], 3), ROWS // ROWS)
    adapter_id = jax.vmap(lambda own, number: shared_out(jax.random.fold_in(own_keys[4], 2), own, number, ROWS, ADAPTERS, 1, CAP, 2))(adapter_id_keys, adapter_id_turns).reshape((ROWS, 1))
    adapter_slot = jax.random.permutation(arg_keys[5], ADAPTERS).astype(jnp.int32)
    return {"hidden_rows": hidden_rows, "down_weight": down_weight, "adapter_down": adapter_down, "adapter_up": adapter_up, "adapter_id": adapter_id, "adapter_slot": adapter_slot}


adapter_scale = 0.5


def reference(hidden_rows, down_weight, adapter_down, adapter_up, adapter_id, adapter_slot):
    slot_of_row = adapter_slot[adapter_id[:, 0]].astype(jnp.int32)
    plain_output_sum = jnp.dot(hidden_rows, down_weight, preferred_element_type=jnp.float32)
    positions = jnp.arange(ROWS, dtype=jnp.int32)

    def per_slot(adapter_output_sum, slot_index):
        sort_keys = jnp.where(slot_of_row == slot_index, positions, positions + ROWS)
        picked = jnp.argsort(sort_keys)[:CAP].astype(jnp.int32)
        is_valid = slot_of_row[picked] == slot_index
        row_block = hidden_rows[picked]
        lowrank = jnp.dot(row_block, adapter_down[slot_index], preferred_element_type=jnp.float32).astype(jnp.bfloat16)
        term_rows = jnp.dot(lowrank, adapter_up[slot_index], preferred_element_type=jnp.float32)
        term_rows = jnp.where(is_valid[:, None], term_rows, jnp.float32(0.0))
        return adapter_output_sum.at[picked].add(term_rows), None

    adapter_output_sum, _ = lax.scan(per_slot, jnp.zeros((ROWS, D), jnp.float32), jnp.arange(ADAPTERS, dtype=jnp.int32))
    return (plain_output_sum + adapter_scale * adapter_output_sum).astype(jnp.bfloat16)
```

```python
import functools
import jax
import jax.numpy as jnp
from jax import lax
from jax.experimental import pallas as pl
from jax.experimental.pallas import tpu as pltpu
from jax.sharding import PartitionSpec as P

adapter_scale = 0.5
MESH = pl.DeviceIdType.MESH


def kernel(
    nt, ng, nr, nk, tile,
    h_ref, w_ref, a_ref, up_ref, id_ref, slot_ref, out_ref,
    wv, av, hbuf, upbuf, acc, racc, rsend, halfbuf, basebuf, rankbuf, lrbuf,
    w_sem, a_sem, own_sem, up_own_sem, flow_send, flow_recv, up_send, up_recv,
    half_send, half_recv, base_send, base_recv, rank_send, rank_recv, lr_send, lr_recv,
):
    t, g, r = lax.axis_index("tensor"), lax.axis_index("group"), lax.axis_index("rep")
    nq = ng * nr
    q = g * nr + r
    per_owner = nt // nq
    rows, depth = h_ref.shape
    width = w_ref.shape[1]
    half = width // nr
    kc = depth // nk
    slots, _, rank = av.shape
    lanes = slots * rank
    up_rows = up_ref.shape[0]
    adapters = slot_ref.shape[0]

    def cols(c):
        return pl.ds(pl.multiple_of(c * kc, 128), kc)

    def half_cols(index):
        return pl.ds(pl.multiple_of(index * half, 128), half)

    def lane_cols(index):
        return pl.ds(pl.multiple_of(index * lanes, 128), lanes)

    def flow(direction, block, c, own):
        source = h_ref.at[:, cols(c)] if own else hbuf.at[block, :, cols(c)]
        target = t + 1 if direction == 0 else t - 1
        return pltpu.make_async_remote_copy(
            src_ref=source, dst_ref=hbuf.at[block, :, cols(c)],
            send_sem=flow_send.at[direction, block, c], recv_sem=flow_recv.at[block, c],
            device_id={"tensor": target}, device_id_type=MESH)

    def w_copy(c):
        part = pl.ds(pl.multiple_of(c * kc, 128), kc)
        return pltpu.make_async_copy(w_ref.at[part], wv.at[part], w_sem.at[c])

    def up_rows_of(index):
        return pl.ds(pl.multiple_of(index * up_rows, 16), up_rows)

    def up_copy(index, source):
        return pltpu.make_async_remote_copy(
            src_ref=up_ref, dst_ref=upbuf.at[up_rows_of(source)],
            send_sem=up_send.at[index], recv_sem=up_recv.at[source],
            device_id={"group": index // nr, "rep": index % nr}, device_id_type=MESH)

    def half_copy(block):
        return pltpu.make_async_remote_copy(
            src_ref=acc.at[block, :, half_cols(1 - r)], dst_ref=halfbuf.at[block],
            send_sem=half_send.at[block], recv_sem=half_recv.at[block],
            device_id={"rep": 1 - r}, device_id_type=MESH)

    def base_copy(block, owner, place):
        return pltpu.make_async_remote_copy(
            src_ref=acc.at[block, :, half_cols(r)], dst_ref=basebuf.at[place, g, r],
            send_sem=base_send.at[block], recv_sem=base_recv.at[place, g * nr + r],
            device_id={"group": owner // nr, "rep": owner % nr}, device_id_type=MESH)

    def rank_copy(block, owner, place):
        return pltpu.make_async_remote_copy(
            src_ref=rsend.at[block], dst_ref=rankbuf.at[place, q],
            send_sem=rank_send.at[block], recv_sem=rank_recv.at[place, q],
            device_id={"group": owner // nr, "rep": owner % nr}, device_id_type=MESH)

    def lr_copy(place, target, source):
        return pltpu.make_async_remote_copy(
            src_ref=lrbuf.at[place, :, lane_cols(source)],
            dst_ref=lrbuf.at[place, :, lane_cols(source)],
            send_sem=lr_send.at[place, target], recv_sem=lr_recv.at[place, source],
            device_id={"tensor": target}, device_id_type=MESH)

    own_copy = pltpu.make_async_copy(h_ref, hbuf.at[t], own_sem)
    a_copy = pltpu.make_async_copy(a_ref, av, a_sem)
    up_own = pltpu.make_async_copy(up_ref, upbuf.at[up_rows_of(q)], up_own_sem)

    own_copy.start()
    a_copy.start()

    @pl.loop(0, nk)
    def _(c):
        w_copy(c).start()

    up_own.start()

    barrier = pltpu.get_barrier_semaphore()

    @pl.loop(0, nt)
    def _(other):
        @pl.when(other != t)
        def _():
            pl.semaphore_signal(barrier, inc=1, device_id={"tensor": other}, device_id_type=MESH)

    @pl.loop(0, nq)
    def _(other):
        @pl.when(other != q)
        def _():
            pl.semaphore_signal(
                barrier, inc=1, device_id={"group": other // nr, "rep": other % nr},
                device_id_type=MESH)

    pl.semaphore_wait(barrier, nt + nq - 2)

    @pl.loop(0, nk)
    def _(c):
        @pl.when(t + 1 < nt)
        def _():
            flow(0, t, c, True).start()

        @pl.when(t > 0)
        def _():
            flow(1, t, c, True).start()

    @pl.loop(0, nq)
    def _(other):
        @pl.when(other != q)
        def _():
            up_copy(other, q).start()

    acc[...] = jnp.zeros_like(acc)
    racc[...] = jnp.zeros_like(racc)

    def multiply(block, c):
        x = hbuf[block, :, cols(c)]

        @pl.loop(0, width // tile)
        def _(n):
            at = pl.ds(pl.multiple_of(n * tile, 128), tile)
            acc[block, :, at] += jnp.dot(
                x, wv[cols(c), at], preferred_element_type=jnp.float32)

        racc[block] += jnp.concatenate(
            [jnp.dot(x, av[s, cols(c), :], preferred_element_type=jnp.float32)
             for s in range(slots)], axis=1)

    def finish(block):
        owner, place = block // per_owner, block % per_owner
        ids = id_ref[pl.ds(pl.multiple_of(block * rows, rows), rows), :]
        row_slot = jnp.zeros_like(ids)
        for adapter in range(adapters):
            row_slot = row_slot + jnp.where(ids == adapter, slot_ref[adapter], 0)
        lane = lax.broadcasted_iota(jnp.int32, (rows, lanes), 1)
        first = (row_slot - t * slots) * rank
        masked = jnp.where((lane >= first) & (lane < first + rank), racc[block], 0.0)

        @pl.when(owner == q)
        def _():
            rankbuf[place, q] = masked

        @pl.when(owner != q)
        def _():
            rsend[block] = masked
            rank_copy(block, owner, place).start()

        half_copy(block).start()

    def combine(block):
        owner, place = block // per_owner, block % per_owner
        half_copy(block).wait_recv()
        value = acc[block, :, half_cols(r)] + halfbuf[block]

        @pl.when(owner == q)
        def _():
            basebuf[place, g, r] = value

        @pl.when(owner != q)
        def _():
            acc[block, :, half_cols(r)] = value
            base_copy(block, owner, place).start()

    own_copy.wait()
    a_copy.wait()

    @pl.loop(0, nk)
    def _(c):
        w_copy(c).wait()
        multiply(t, c)

    finish(t)
    combine(t)

    @pl.loop(1, nt)
    def _(step):
        left, right = t - step, t + step
        has_left, has_right = left >= 0, right < nt

        @pl.loop(0, nk)
        def _(c):
            @pl.when(has_left)
            def _():
                flow(0, left, c, False).wait_recv()

                @pl.when(t + 1 < nt)
                def _():
                    flow(0, left, c, False).start()

            @pl.when(has_right)
            def _():
                flow(1, right, c, False).wait_recv()

                @pl.when(t > 0)
                def _():
                    flow(1, right, c, False).start()

            @pl.when(has_left)
            def _():
                multiply(left, c)

            @pl.when(has_right)
            def _():
                multiply(right, c)

        @pl.when(has_left)
        def _():
            finish(left)

        @pl.when(has_right)
        def _():
            finish(right)

        @pl.when(has_left)
        def _():
            combine(left)

        @pl.when(has_right)
        def _():
            combine(right)

    @pl.loop(0, per_owner)
    def _(place):
        @pl.loop(0, nq)
        def _(other):
            @pl.when(other != q)
            def _():
                pltpu.make_async_remote_copy(
                    src_ref=rsend.at[0], dst_ref=rankbuf.at[place, other],
                    send_sem=rank_send.at[0], recv_sem=rank_recv.at[place, other],
                    device_id={"rep": 1 - r}, device_id_type=MESH).wait_recv()

        total = rankbuf[place, 0]
        for other in range(1, nq):
            total = total + rankbuf[place, other]
        lrbuf[place, :, lane_cols(t)] = total.astype(jnp.bfloat16)

        @pl.loop(0, nt)
        def _(other):
            @pl.when(other != t)
            def _():
                lr_copy(place, other, t).start()

    up_own.wait()

    @pl.loop(0, nq)
    def _(other):
        @pl.when(other != q)
        def _():
            up_copy(other, other).wait_recv()

    @pl.loop(0, per_owner)
    def _(place):
        @pl.loop(0, nq)
        def _(other):
            @pl.when(other != q)
            def _():
                pltpu.make_async_remote_copy(
                    src_ref=halfbuf.at[0], dst_ref=basebuf.at[place, other // nr, other % nr],
                    send_sem=base_send.at[0], recv_sem=base_recv.at[place, other],
                    device_id={"rep": 1 - r}, device_id_type=MESH).wait_recv()

        @pl.loop(0, nt)
        def _(other):
            @pl.when(other != t)
            def _():
                lr_copy(place, other, other).wait_recv()

        spread = lrbuf[place]
        out_rows = pl.ds(pl.multiple_of(place * rows, rows), rows)
        for part in range(nr):
            total = basebuf[place, 0, part]
            for other in range(1, ng):
                total = total + basebuf[place, other, part]
            at = slice(part * half, (part + 1) * half)
            delta = jnp.dot(spread, upbuf[:, at], preferred_element_type=jnp.float32)
            out_ref[out_rows, at] = (total + adapter_scale * delta).astype(jnp.bfloat16)

    @pl.loop(0, nk)
    def _(c):
        @pl.when(t + 1 < nt)
        def _():
            flow(0, t, c, True).wait_send()

            @pl.loop(0, t)
            def _(block):
                flow(0, block, c, False).wait_send()

        @pl.when(t > 0)
        def _():
            flow(1, t, c, True).wait_send()

            @pl.loop(t + 1, nt)
            def _(block):
                flow(1, block, c, False).wait_send()

    @pl.loop(0, nq)
    def _(other):
        @pl.when(other != q)
        def _():
            up_copy(other, q).wait_send()

    @pl.loop(0, nt)
    def _(block):
        owner, place = block // per_owner, block % per_owner
        half_copy(block).wait_send()

        @pl.when(owner != q)
        def _():
            base_copy(block, owner, place).wait_send()
            rank_copy(block, owner, place).wait_send()

    @pl.loop(0, per_owner)
    def _(place):
        @pl.loop(0, nt)
        def _(other):
            @pl.when(other != t)
            def _():
                lr_copy(place, other, t).wait_send()


def on_device(hidden_rows, down_weight, adapter_down, adapter_up, adapter_id, adapter_slot):
    nt, ng, nr = (lax.axis_size(name) for name in ("tensor", "group", "rep"))
    nq = ng * nr
    rows, depth = hidden_rows.shape
    width = down_weight.shape[1]
    slots, _, rank = adapter_down.shape
    up_rows = adapter_up.shape[0] * rank
    lanes = slots * rank
    per_owner = nt // nq
    nk = next(n for n in (7, 2, 1) if depth % (n * 128) == 0 and nt * n <= 64)
    tile = min(512, width)
    up_flat = adapter_up.reshape(up_rows, width)
    anywhere = pl.BlockSpec(memory_space=pl.ANY)
    f32, bf16 = jnp.float32, jnp.bfloat16
    dma = pltpu.SemaphoreType.DMA
    return pl.pallas_call(
        functools.partial(kernel, nt, ng, nr, nk, tile),
        out_shape=jax.ShapeDtypeStruct((per_owner * rows, width), bf16),
        in_specs=[anywhere] * 4 + [
            pl.BlockSpec(memory_space=pltpu.VMEM), pl.BlockSpec(memory_space=pltpu.SMEM)],
        out_specs=pl.BlockSpec(memory_space=pltpu.VMEM),
        scratch_shapes=[
            pltpu.VMEM((depth, width), bf16),
            pltpu.VMEM((slots, depth, rank), bf16),
            pltpu.VMEM((nt, rows, depth), bf16),
            pltpu.VMEM((nq * up_rows, width), bf16),
            pltpu.VMEM((nt, rows, width), f32),
            pltpu.VMEM((nt, rows, lanes), f32),
            pltpu.VMEM((nt, rows, lanes), f32),
            pltpu.VMEM((nt, rows, width // nr), f32),
            pltpu.VMEM((per_owner, ng, nr, rows, width // nr), f32),
            pltpu.VMEM((per_owner, nq, rows, lanes), f32),
            pltpu.VMEM((per_owner, rows, nt * lanes), bf16),
            dma((nk,)), dma, dma, dma,
            dma((2, nt, nk)), dma((nt, nk)), dma((nq,)), dma((nq,)),
            dma((nt,)), dma((nt,)), dma((nt,)), dma((per_owner, nq)),
            dma((nt,)), dma((per_owner, nq)), dma((per_owner, nt)), dma((per_owner, nt)),
        ],
        compiler_params=pltpu.CompilerParams(
            collective_id=0, has_side_effects=True, vmem_limit_bytes=58 * 2**20),
    )(hidden_rows, down_weight, adapter_down, up_flat, adapter_id, adapter_slot)


def solution(mesh):
    placed = (
        P(("parts", "tensor"), ("group", "rep")),
        P(("group", "rep"), "tensor"),
        P("tensor", ("group", "rep"), None),
        P(("group", "rep"), None, "tensor"),
        P("parts", None),
        P(),
    )
    return jax.shard_map(
        on_device,
        mesh=mesh,
        in_specs=placed,
        out_specs=P(("parts", "group", "rep"), "tensor"),
        check_vma=False,
    )
```

```python
import functools
import jax
import jax.numpy as jnp
from jax import lax
from jax.experimental import pallas as pl
from jax.experimental.pallas import tpu as pltpu
from jax.sharding import PartitionSpec as P

adapter_scale = 0.5
MESH = pl.DeviceIdType.MESH


def kernel(
    nt, ng, nr, nk, tile, rank,
    h_ref, w_ref, a_ref, up_ref, id_ref, slot_ref, out_ref,
    wv, av, hbuf, upbuf, acc, racc, chosen, rsend, halfbuf, basebuf, rankbuf, lrbuf,
    w_sem, a_sem, own_sem, up_own_sem, flow_send, flow_recv, up_send, up_recv,
    half_send, half_recv, base_send, base_recv, rank_send, rank_recv, lr_send, lr_recv,
):
    t, g, r = lax.axis_index("tensor"), lax.axis_index("group"), lax.axis_index("rep")
    nq = ng * nr
    q = g * nr + r
    per_owner = nt // nq
    rows, depth = h_ref.shape
    width = w_ref.shape[1]
    half = width // nr
    kc = depth // nk
    lanes = av.shape[0]
    slots = lanes // rank
    up_rows = up_ref.shape[0]
    adapters = slot_ref.shape[0]

    def cols(c):
        return pl.ds(pl.multiple_of(c * kc, 128), kc)

    def half_cols(index):
        return pl.ds(pl.multiple_of(index * half, 128), half)

    def lane_cols(index):
        return pl.ds(pl.multiple_of(index * lanes, 128), lanes)

    def flow(direction, block, c, own):
        source = h_ref.at[:, cols(c)] if own else hbuf.at[block, :, cols(c)]
        target = t + 1 if direction == 0 else t - 1
        return pltpu.make_async_remote_copy(
            src_ref=source, dst_ref=hbuf.at[block, :, cols(c)],
            send_sem=flow_send.at[direction, block, c], recv_sem=flow_recv.at[block, c],
            device_id={"tensor": target}, device_id_type=MESH)

    def w_copy(c):
        part = pl.ds(pl.multiple_of(c * kc, 128), kc)
        return pltpu.make_async_copy(w_ref.at[part], wv.at[part], w_sem.at[c])

    def up_rows_of(index):
        return pl.ds(pl.multiple_of(index * up_rows, 16), up_rows)

    def up_copy(index, source):
        return pltpu.make_async_remote_copy(
            src_ref=up_ref, dst_ref=upbuf.at[up_rows_of(source)],
            send_sem=up_send.at[index], recv_sem=up_recv.at[source],
            device_id={"group": index // nr, "rep": index % nr}, device_id_type=MESH)

    def half_copy(block):
        return pltpu.make_async_remote_copy(
            src_ref=acc.at[block, :, half_cols(1 - r)], dst_ref=halfbuf.at[block],
            send_sem=half_send.at[block], recv_sem=half_recv.at[block],
            device_id={"rep": 1 - r}, device_id_type=MESH)

    def base_copy(block, owner, place):
        return pltpu.make_async_remote_copy(
            src_ref=acc.at[block, :, half_cols(r)], dst_ref=basebuf.at[place, g, r],
            send_sem=base_send.at[block], recv_sem=base_recv.at[place, g * nr + r],
            device_id={"group": owner // nr, "rep": owner % nr}, device_id_type=MESH)

    def rank_copy(block, owner, place):
        return pltpu.make_async_remote_copy(
            src_ref=rsend.at[block], dst_ref=rankbuf.at[place, q],
            send_sem=rank_send.at[block], recv_sem=rank_recv.at[place, q],
            device_id={"group": owner // nr, "rep": owner % nr}, device_id_type=MESH)

    def lr_copy(place, target, source):
        return pltpu.make_async_remote_copy(
            src_ref=lrbuf.at[place, :, lane_cols(source)],
            dst_ref=lrbuf.at[place, :, lane_cols(source)],
            send_sem=lr_send.at[place, target], recv_sem=lr_recv.at[place, source],
            device_id={"tensor": target}, device_id_type=MESH)

    own_copy = pltpu.make_async_copy(h_ref, hbuf.at[t], own_sem)
    a_copy = pltpu.make_async_copy(a_ref, av, a_sem)
    up_own = pltpu.make_async_copy(up_ref, upbuf.at[up_rows_of(q)], up_own_sem)

    own_copy.start()
    a_copy.start()

    @pl.loop(0, nk)
    def _(c):
        w_copy(c).start()

    up_own.start()

    barrier = pltpu.get_barrier_semaphore()

    @pl.loop(0, nt)
    def _(other):
        @pl.when(other != t)
        def _():
            pl.semaphore_signal(barrier, inc=1, device_id={"tensor": other}, device_id_type=MESH)

    @pl.loop(0, nq)
    def _(other):
        @pl.when(other != q)
        def _():
            pl.semaphore_signal(
                barrier, inc=1, device_id={"group": other // nr, "rep": other % nr},
                device_id_type=MESH)

    pl.semaphore_wait(barrier, nt + nq - 2)

    @pl.loop(0, nk)
    def _(c):
        @pl.when(t + 1 < nt)
        def _():
            flow(0, t, c, True).start()

        @pl.when(t > 0)
        def _():
            flow(1, t, c, True).start()

    @pl.loop(0, nq)
    def _(other):
        @pl.when(other != q)
        def _():
            up_copy(other, q).start()

    acc[...] = jnp.zeros_like(acc)
    racc[...] = jnp.zeros_like(racc)
    ids = id_ref[...]
    row_slot = jnp.zeros_like(ids)
    for adapter in range(adapters):
        row_slot = row_slot + jnp.where(ids == adapter, slot_ref[adapter], 0)
    lane = lax.broadcasted_iota(jnp.int32, (lanes, nt * rows), 0)
    first = jnp.broadcast_to((row_slot - t * slots) * rank, (lanes, nt * rows))
    named = jnp.where((lane >= first) & (lane < first + rank), 1.0, 0.0).astype(jnp.float32)
    chosen[...] = jnp.transpose(named).reshape(nt, rows, lanes)

    def multiply(block, c):
        x = hbuf[block, :, cols(c)]

        @pl.loop(0, width // tile)
        def _(n):
            at = pl.ds(pl.multiple_of(n * tile, 128), tile)
            acc[block, :, at] += jnp.dot(
                x, wv[cols(c), at], preferred_element_type=jnp.float32)

        racc[block] += lax.dot_general(
            x, av[:, cols(c)], (((1,), (1,)), ((), ())), preferred_element_type=jnp.float32)

    def finish(block):
        owner, place = block // per_owner, block % per_owner
        masked = jnp.where(chosen[block] > 0.5, racc[block], 0.0)

        @pl.when(owner == q)
        def _():
            rankbuf[place, q] = masked

        @pl.when(owner != q)
        def _():
            rsend[block] = masked
            rank_copy(block, owner, place).start()

        half_copy(block).start()

    def combine(block):
        owner, place = block // per_owner, block % per_owner
        half_copy(block).wait_recv()
        value = acc[block, :, half_cols(r)] + halfbuf[block]

        @pl.when(owner == q)
        def _():
            basebuf[place, g, r] = value

        @pl.when(owner != q)
        def _():
            acc[block, :, half_cols(r)] = value
            base_copy(block, owner, place).start()

    own_copy.wait()
    a_copy.wait()

    @pl.loop(0, nk)
    def _(c):
        w_copy(c).wait()
        multiply(t, c)

    finish(t)
    combine(t)

    @pl.loop(1, nt)
    def _(step):
        left, right = t - step, t + step
        has_left, has_right = left >= 0, right < nt

        @pl.loop(0, nk)
        def _(c):
            @pl.when(has_left)
            def _():
                flow(0, left, c, False).wait_recv()

                @pl.when(t + 1 < nt)
                def _():
                    flow(0, left, c, False).start()

            @pl.when(has_right)
            def _():
                flow(1, right, c, False).wait_recv()

                @pl.when(t > 0)
                def _():
                    flow(1, right, c, False).start()

            @pl.when(has_left)
            def _():
                multiply(left, c)

            @pl.when(has_right)
            def _():
                multiply(right, c)

        @pl.when(has_left)
        def _():
            finish(left)

        @pl.when(has_right)
        def _():
            finish(right)

        @pl.when(has_left)
        def _():
            combine(left)

        @pl.when(has_right)
        def _():
            combine(right)

    @pl.loop(0, per_owner)
    def _(place):
        @pl.loop(0, nq)
        def _(other):
            @pl.when(other != q)
            def _():
                pltpu.make_async_remote_copy(
                    src_ref=rsend.at[0], dst_ref=rankbuf.at[place, other],
                    send_sem=rank_send.at[0], recv_sem=rank_recv.at[place, other],
                    device_id={"rep": 1 - r}, device_id_type=MESH).wait_recv()

        total = rankbuf[place, 0]
        for other in range(1, nq):
            total = total + rankbuf[place, other]
        lrbuf[place, :, lane_cols(t)] = total.astype(jnp.bfloat16)

        @pl.loop(0, nt)
        def _(other):
            @pl.when(other != t)
            def _():
                lr_copy(place, other, t).start()

    up_own.wait()

    @pl.loop(0, nq)
    def _(other):
        @pl.when(other != q)
        def _():
            up_copy(other, other).wait_recv()

    @pl.loop(0, per_owner)
    def _(place):
        @pl.loop(0, nq)
        def _(other):
            @pl.when(other != q)
            def _():
                pltpu.make_async_remote_copy(
                    src_ref=halfbuf.at[0], dst_ref=basebuf.at[place, other // nr, other % nr],
                    send_sem=base_send.at[0], recv_sem=base_recv.at[place, other],
                    device_id={"rep": 1 - r}, device_id_type=MESH).wait_recv()

        @pl.loop(0, nt)
        def _(other):
            @pl.when(other != t)
            def _():
                lr_copy(place, other, other).wait_recv()

        spread = lrbuf[place]
        out_rows = pl.ds(pl.multiple_of(place * rows, rows), rows)
        for part in range(nr):
            total = basebuf[place, 0, part]
            for other in range(1, ng):
                total = total + basebuf[place, other, part]
            at = slice(part * half, (part + 1) * half)
            delta = jnp.dot(spread, upbuf[:, at], preferred_element_type=jnp.float32)
            out_ref[out_rows, at] = (total + adapter_scale * delta).astype(jnp.bfloat16)

    @pl.loop(0, nk)
    def _(c):
        @pl.when(t + 1 < nt)
        def _():
            flow(0, t, c, True).wait_send()

            @pl.loop(0, t)
            def _(block):
                flow(0, block, c, False).wait_send()

        @pl.when(t > 0)
        def _():
            flow(1, t, c, True).wait_send()

            @pl.loop(t + 1, nt)
            def _(block):
                flow(1, block, c, False).wait_send()

    @pl.loop(0, nq)
    def _(other):
        @pl.when(other != q)
        def _():
            up_copy(other, q).wait_send()

    @pl.loop(0, nt)
    def _(block):
        owner, place = block // per_owner, block % per_owner
        half_copy(block).wait_send()

        @pl.when(owner != q)
        def _():
            base_copy(block, owner, place).wait_send()
            rank_copy(block, owner, place).wait_send()

    @pl.loop(0, per_owner)
    def _(place):
        @pl.loop(0, nt)
        def _(other):
            @pl.when(other != t)
            def _():
                lr_copy(place, other, t).wait_send()


def on_device(hidden_rows, down_weight, adapter_down, adapter_up, adapter_id, adapter_slot):
    nt, ng, nr = (lax.axis_size(name) for name in ("tensor", "group", "rep"))
    nq = ng * nr
    rows, depth = hidden_rows.shape
    width = down_weight.shape[1]
    slots, _, rank = adapter_down.shape
    up_rows = adapter_up.shape[0] * rank
    lanes = slots * rank
    per_owner = nt // nq
    nk = next(n for n in (7, 2, 1) if depth % (n * 128) == 0 and nt * n <= 64)
    tile = min(512, width)
    down_flat = jnp.swapaxes(adapter_down, 1, 2).reshape(lanes, depth)
    up_flat = adapter_up.reshape(up_rows, width)
    anywhere = pl.BlockSpec(memory_space=pl.ANY)
    f32, bf16 = jnp.float32, jnp.bfloat16
    dma = pltpu.SemaphoreType.DMA
    return pl.pallas_call(
        functools.partial(kernel, nt, ng, nr, nk, tile, rank),
        out_shape=jax.ShapeDtypeStruct((per_owner * rows, width), bf16),
        in_specs=[anywhere] * 4 + [
            pl.BlockSpec(memory_space=pltpu.VMEM), pl.BlockSpec(memory_space=pltpu.SMEM)],
        out_specs=pl.BlockSpec(memory_space=pltpu.VMEM),
        scratch_shapes=[
            pltpu.VMEM((depth, width), bf16),
            pltpu.VMEM((lanes, depth), bf16),
            pltpu.VMEM((nt, rows, depth), bf16),
            pltpu.VMEM((nq * up_rows, width), bf16),
            pltpu.VMEM((nt, rows, width), f32),
            pltpu.VMEM((nt, rows, lanes), f32),
            pltpu.VMEM((nt, rows, lanes), f32),
            pltpu.VMEM((nt, rows, lanes), f32),
            pltpu.VMEM((nt, rows, width // nr), f32),
            pltpu.VMEM((per_owner, ng, nr, rows, width // nr), f32),
            pltpu.VMEM((per_owner, nq, rows, lanes), f32),
            pltpu.VMEM((per_owner, rows, nt * lanes), bf16),
            dma((nk,)), dma, dma, dma,
            dma((2, nt, nk)), dma((nt, nk)), dma((nq,)), dma((nq,)),
            dma((nt,)), dma((nt,)), dma((nt,)), dma((per_owner, nq)),
            dma((nt,)), dma((per_owner, nq)), dma((per_owner, nt)), dma((per_owner, nt)),
        ],
        compiler_params=pltpu.CompilerParams(
            collective_id=0, has_side_effects=True, vmem_limit_bytes=58 * 2**20),
    )(hidden_rows, down_weight, down_flat, up_flat, adapter_id.reshape(1, -1), adapter_slot)


def solution(mesh):
    placed = (
        P(("parts", "tensor"), ("group", "rep")),
        P(("group", "rep"), "tensor"),
        P("tensor", ("group", "rep"), None),
        P(("group", "rep"), None, "tensor"),
        P("parts", None),
        P(),
    )
    return jax.shard_map(
        on_device,
        mesh=mesh,
        in_specs=placed,
        out_specs=P(("parts", "group", "rep"), "tensor"),
        check_vma=False,
    )
```

```python
import functools
import jax
import jax.numpy as jnp
from jax import lax
from jax.experimental import pallas as pl
from jax.experimental.pallas import tpu as pltpu
from jax.sharding import PartitionSpec as P

adapter_scale = 0.5
MESH = pl.DeviceIdType.MESH


def kernel(
    nt, ng, nr, nk, tile, rank,
    h_ref, w_ref, a_ref, up_ref, id_ref, slot_ref, out_ref,
    wv, av, hbuf, upbuf, acc, racc, chosen, rsend, halfbuf, basebuf, rankbuf, lrbuf,
    w_sem, a_sem, own_sem, up_own_sem, flow_send, flow_recv, up_send, up_recv,
    half_send, half_recv, base_send, base_recv, rank_send, rank_recv, lr_send, lr_recv,
):
    t, g, r = lax.axis_index("tensor"), lax.axis_index("group"), lax.axis_index("rep")
    nq = ng * nr
    q = g * nr + r
    per_owner = nt // nq
    rows, depth = h_ref.shape
    width = w_ref.shape[1]
    half = width // nr
    kc = depth // nk
    lanes = av.shape[0]
    slots = lanes // rank
    up_rows = up_ref.shape[0]
    adapters = slot_ref.shape[0]

    def cols(c):
        return pl.ds(pl.multiple_of(c * kc, 128), kc)

    def half_cols(index):
        return pl.ds(pl.multiple_of(index * half, 128), half)

    def lane_cols(index):
        return pl.ds(pl.multiple_of(index * lanes, 128), lanes)

    def flow(direction, block, c):
        target = t + 1 if direction == 0 else t - 1
        return pltpu.make_async_remote_copy(
            src_ref=hbuf.at[block, c], dst_ref=hbuf.at[block, c],
            send_sem=flow_send.at[direction, block, c], recv_sem=flow_recv.at[block, c],
            device_id={"tensor": target}, device_id_type=MESH)

    def w_copy(c):
        part = pl.ds(pl.multiple_of(c * kc, 128), kc)
        return pltpu.make_async_copy(w_ref.at[part], wv.at[part], w_sem.at[c])

    def up_rows_of(index):
        return pl.ds(pl.multiple_of(index * up_rows, 16), up_rows)

    def up_copy(index, source):
        return pltpu.make_async_remote_copy(
            src_ref=up_ref, dst_ref=upbuf.at[up_rows_of(source)],
            send_sem=up_send.at[index], recv_sem=up_recv.at[source],
            device_id={"group": index // nr, "rep": index % nr}, device_id_type=MESH)

    def half_copy(block):
        return pltpu.make_async_remote_copy(
            src_ref=acc.at[block, :, half_cols(1 - r)], dst_ref=halfbuf.at[block],
            send_sem=half_send.at[block], recv_sem=half_recv.at[block],
            device_id={"rep": 1 - r}, device_id_type=MESH)

    def base_copy(block, owner, place):
        return pltpu.make_async_remote_copy(
            src_ref=acc.at[block, :, half_cols(r)], dst_ref=basebuf.at[place, g, r],
            send_sem=base_send.at[block], recv_sem=base_recv.at[place, g * nr + r],
            device_id={"group": owner // nr, "rep": owner % nr}, device_id_type=MESH)

    def rank_copy(block, owner, place):
        return pltpu.make_async_remote_copy(
            src_ref=rsend.at[block], dst_ref=rankbuf.at[place, q],
            send_sem=rank_send.at[block], recv_sem=rank_recv.at[place, q],
            device_id={"group": owner // nr, "rep": owner % nr}, device_id_type=MESH)

    def lr_copy(place, target, source):
        return pltpu.make_async_remote_copy(
            src_ref=lrbuf.at[place, :, lane_cols(source)],
            dst_ref=lrbuf.at[place, :, lane_cols(source)],
            send_sem=lr_send.at[place, target], recv_sem=lr_recv.at[place, source],
            device_id={"tensor": target}, device_id_type=MESH)

    def own_copy(c):
        return pltpu.make_async_copy(h_ref.at[:, cols(c)], hbuf.at[t, c], own_sem.at[c])

    a_copy = pltpu.make_async_copy(a_ref, av, a_sem)
    up_own = pltpu.make_async_copy(up_ref, upbuf.at[up_rows_of(q)], up_own_sem)

    @pl.loop(0, nk)
    def _(c):
        own_copy(c).start()

    a_copy.start()

    @pl.loop(0, nk)
    def _(c):
        w_copy(c).start()

    up_own.start()

    barrier = pltpu.get_barrier_semaphore()

    @pl.loop(0, nt)
    def _(other):
        @pl.when(other != t)
        def _():
            pl.semaphore_signal(barrier, inc=1, device_id={"tensor": other}, device_id_type=MESH)

    @pl.loop(0, nq)
    def _(other):
        @pl.when(other != q)
        def _():
            pl.semaphore_signal(
                barrier, inc=1, device_id={"group": other // nr, "rep": other % nr},
                device_id_type=MESH)

    pl.semaphore_wait(barrier, nt + nq - 2)

    @pl.loop(0, nk)
    def _(c):
        own_copy(c).wait()

        @pl.when(t + 1 < nt)
        def _():
            flow(0, t, c).start()

        @pl.when(t > 0)
        def _():
            flow(1, t, c).start()

    @pl.loop(0, nq)
    def _(other):
        @pl.when(other != q)
        def _():
            up_copy(other, q).start()

    acc[...] = jnp.zeros_like(acc)
    racc[...] = jnp.zeros_like(racc)
    ids = id_ref[...]
    row_slot = jnp.zeros_like(ids)
    for adapter in range(adapters):
        row_slot = row_slot + jnp.where(ids == adapter, slot_ref[adapter], 0)
    lane = lax.broadcasted_iota(jnp.int32, (lanes, nt * rows), 0)
    first = jnp.broadcast_to((row_slot - t * slots) * rank, (lanes, nt * rows))
    named = jnp.where((lane >= first) & (lane < first + rank), 1.0, 0.0).astype(jnp.float32)
    chosen[...] = jnp.transpose(named).reshape(nt, rows, lanes)

    def multiply(block, c):
        x = hbuf[block, c]

        @pl.loop(0, width // tile)
        def _(n):
            at = pl.ds(pl.multiple_of(n * tile, 128), tile)
            acc[block, :, at] += jnp.dot(
                x, wv[cols(c), at], preferred_element_type=jnp.float32)

        racc[block] += lax.dot_general(
            x, av[:, cols(c)], (((1,), (1,)), ((), ())), preferred_element_type=jnp.float32)

    def finish(block):
        owner, place = block // per_owner, block % per_owner
        masked = jnp.where(chosen[block] > 0.5, racc[block], 0.0)

        @pl.when(owner == q)
        def _():
            rankbuf[place, q] = masked

        @pl.when(owner != q)
        def _():
            rsend[block] = masked
            rank_copy(block, owner, place).start()

        half_copy(block).start()

    def combine(block):
        owner, place = block // per_owner, block % per_owner
        half_copy(block).wait_recv()
        value = acc[block, :, half_cols(r)] + halfbuf[block]

        @pl.when(owner == q)
        def _():
            basebuf[place, g, r] = value

        @pl.when(owner != q)
        def _():
            acc[block, :, half_cols(r)] = value
            base_copy(block, owner, place).start()

    a_copy.wait()

    @pl.loop(0, nk)
    def _(c):
        w_copy(c).wait()
        multiply(t, c)

    finish(t)
    combine(t)

    @pl.loop(1, nt)
    def _(step):
        left, right = t - step, t + step
        has_left, has_right = left >= 0, right < nt

        @pl.loop(0, nk)
        def _(c):
            @pl.when(has_left)
            def _():
                flow(0, left, c).wait_recv()

                @pl.when(t + 1 < nt)
                def _():
                    flow(0, left, c).start()

            @pl.when(has_right)
            def _():
                flow(1, right, c).wait_recv()

                @pl.when(t > 0)
                def _():
                    flow(1, right, c).start()

            @pl.when(has_left)
            def _():
                multiply(left, c)

            @pl.when(has_right)
            def _():
                multiply(right, c)

        @pl.when(has_left)
        def _():
            finish(left)

        @pl.when(has_right)
        def _():
            finish(right)

        @pl.when(has_left)
        def _():
            combine(left)

        @pl.when(has_right)
        def _():
            combine(right)

    @pl.loop(0, per_owner)
    def _(place):
        @pl.loop(0, nq)
        def _(other):
            @pl.when(other != q)
            def _():
                pltpu.make_async_remote_copy(
                    src_ref=rsend.at[0], dst_ref=rankbuf.at[place, other],
                    send_sem=rank_send.at[0], recv_sem=rank_recv.at[place, other],
                    device_id={"rep": 1 - r}, device_id_type=MESH).wait_recv()

        total = rankbuf[place, 0]
        for other in range(1, nq):
            total = total + rankbuf[place, other]
        lrbuf[place, :, lane_cols(t)] = total.astype(jnp.bfloat16)

        @pl.loop(0, nt)
        def _(other):
            @pl.when(other != t)
            def _():
                lr_copy(place, other, t).start()

    up_own.wait()

    @pl.loop(0, nq)
    def _(other):
        @pl.when(other != q)
        def _():
            up_copy(other, other).wait_recv()

    @pl.loop(0, per_owner)
    def _(place):
        @pl.loop(0, nq)
        def _(other):
            @pl.when(other != q)
            def _():
                pltpu.make_async_remote_copy(
                    src_ref=halfbuf.at[0], dst_ref=basebuf.at[place, other // nr, other % nr],
                    send_sem=base_send.at[0], recv_sem=base_recv.at[place, other],
                    device_id={"rep": 1 - r}, device_id_type=MESH).wait_recv()

        @pl.loop(0, nt)
        def _(other):
            @pl.when(other != t)
            def _():
                lr_copy(place, other, other).wait_recv()

        spread = lrbuf[place]
        out_rows = pl.ds(pl.multiple_of(place * rows, rows), rows)
        for part in range(nr):
            total = basebuf[place, 0, part]
            for other in range(1, ng):
                total = total + basebuf[place, other, part]
            at = slice(part * half, (part + 1) * half)
            delta = jnp.dot(spread, upbuf[:, at], preferred_element_type=jnp.float32)
            out_ref[out_rows, at] = total + adapter_scale * delta

    @pl.loop(0, nk)
    def _(c):
        @pl.when(t + 1 < nt)
        def _():
            flow(0, t, c).wait_send()

            @pl.loop(0, t)
            def _(block):
                flow(0, block, c).wait_send()

        @pl.when(t > 0)
        def _():
            flow(1, t, c).wait_send()

            @pl.loop(t + 1, nt)
            def _(block):
                flow(1, block, c).wait_send()

    @pl.loop(0, nq)
    def _(other):
        @pl.when(other != q)
        def _():
            up_copy(other, q).wait_send()

    @pl.loop(0, nt)
    def _(block):
        owner, place = block // per_owner, block % per_owner
        half_copy(block).wait_send()

        @pl.when(owner != q)
        def _():
            base_copy(block, owner, place).wait_send()
            rank_copy(block, owner, place).wait_send()

    @pl.loop(0, per_owner)
    def _(place):
        @pl.loop(0, nt)
        def _(other):
            @pl.when(other != t)
            def _():
                lr_copy(place, other, t).wait_send()


def on_device(hidden_rows, down_weight, adapter_down, adapter_up, adapter_id, adapter_slot):
    nt, ng, nr = (lax.axis_size(name) for name in ("tensor", "group", "rep"))
    nq = ng * nr
    rows, depth = hidden_rows.shape
    width = down_weight.shape[1]
    slots, _, rank = adapter_down.shape
    up_rows = adapter_up.shape[0] * rank
    lanes = slots * rank
    per_owner = nt // nq
    nk = next(n for n in (7, 2, 1) if depth % (n * 128) == 0 and nt * n <= 64)
    tile = min(512, width)
    down_flat = jnp.swapaxes(adapter_down, 1, 2).reshape(lanes, depth)
    up_flat = adapter_up.reshape(up_rows, width)
    anywhere = pl.BlockSpec(memory_space=pl.ANY)
    f32, bf16 = jnp.float32, jnp.bfloat16
    dma = pltpu.SemaphoreType.DMA
    return pl.pallas_call(
        functools.partial(kernel, nt, ng, nr, nk, tile, rank),
        out_shape=jax.ShapeDtypeStruct((per_owner * rows, width), f32),
        in_specs=[anywhere] * 4 + [
            pl.BlockSpec(memory_space=pltpu.VMEM), pl.BlockSpec(memory_space=pltpu.SMEM)],
        out_specs=pl.BlockSpec(memory_space=pltpu.VMEM),
        scratch_shapes=[
            pltpu.VMEM((depth, width), bf16),
            pltpu.VMEM((lanes, depth), bf16),
            pltpu.VMEM((nt, nk, rows, depth // nk), bf16),
            pltpu.VMEM((nq * up_rows, width), bf16),
            pltpu.VMEM((nt, rows, width), f32),
            pltpu.VMEM((nt, rows, lanes), f32),
            pltpu.VMEM((nt, rows, lanes), f32),
            pltpu.VMEM((nt, rows, lanes), f32),
            pltpu.VMEM((nt, rows, width // nr), f32),
            pltpu.VMEM((per_owner, ng, nr, rows, width // nr), f32),
            pltpu.VMEM((per_owner, nq, rows, lanes), f32),
            pltpu.VMEM((per_owner, rows, nt * lanes), bf16),
            dma((nk,)), dma, dma((nk,)), dma,
            dma((2, nt, nk)), dma((nt, nk)), dma((nq,)), dma((nq,)),
            dma((nt,)), dma((nt,)), dma((nt,)), dma((per_owner, nq)),
            dma((nt,)), dma((per_owner, nq)), dma((per_owner, nt)), dma((per_owner, nt)),
        ],
        compiler_params=pltpu.CompilerParams(
            collective_id=0, has_side_effects=True, vmem_limit_bytes=58 * 2**20),
    )(hidden_rows, down_weight, down_flat, up_flat, adapter_id.reshape(1, -1), adapter_slot).astype(bf16)


def solution(mesh):
    placed = (
        P(("parts", "tensor"), ("group", "rep")),
        P(("group", "rep"), "tensor"),
        P("tensor", ("group", "rep"), None),
        P(("group", "rep"), None, "tensor"),
        P("parts", None),
        P(),
    )
    return jax.shard_map(
        on_device,
        mesh=mesh,
        in_specs=placed,
        out_specs=P(("parts", "group", "rep"), "tensor"),
        check_vma=False,
    )
```
